256 devices in a mesh: rows: 32 (over y, x, core), lists: 8 (over z).
Axes of the slice: x: 4, y: 4, z: 8, core: 2. Of those that a mesh axis runs over, the one named last changes fastest.
Arguments:
- samples: bfloat16 [32768, 256], P('rows'), may hold values from -100 to 100
- centers: bfloat16 [32768, 256], P('lists'), may hold values from -4 to 4
Outputs:
- assignment: bfloat16 [32768, 32768], P('rows', 'lists')
- new_centers: float32 [32768, 256], P(('lists', 'rows'))
The draws below stay inside these ranges and needn't reach their ends.
All inputs are finite; a program needn't handle non-finite values.
Results may differ from the reference program's by a relative error of at most 0.0054.
Values may be sent and summed in bfloat16 or wider, within the bound.
A program may use at most 128 MiB of HBM per device.

```python
import jax
import jax.numpy as jnp
from jax import lax

D = 256
ITERS = 3
KLISTS = 32768
NROWS = 32768


def replicated_centers(key):
    return jax.random.truncated_normal(key, -4.0, 4.0, (KLISTS, D), jnp.float32)


def draw_centers(key, part):
    base = replicated_centers(key)
    return base.astype(jnp.bfloat16)


def draw_samples(key, part):
    base = replicated_centers(key)
    key = jax.random.fold_in(key, 7)
    key_index, key_noise = jax.random.split(key, 2)
    picked = jax.random.randint(key_index, (NROWS,), 0, KLISTS)
    noise = jax.random.truncated_normal(key_noise, -4.0, 4.0, (NROWS, D), jnp.float32)
    value_entries = base[picked] + noise
    return value_entries.astype(jnp.bfloat16)


def setup_inputs(seed: int = 0) -> dict:
    seeds = jax.random.split(jax.random.key(seed), 3)
    return {
        "samples": draw_samples(jax.random.fold_in(seeds[2], 71), 0),
        "centers": draw_centers(jax.random.fold_in(seeds[2], 71), 0),
    }


SOFTMAX_TEMP_VALUE = 0.03

def unit_norm(value_entries):
    wide = value_entries.astype(jnp.float32)
    return (wide / jnp.sqrt(lax.optimization_barrier(jnp.sum(wide * wide, 1, keepdims=True)) + 1e-06)).astype(jnp.bfloat16)

def reference(samples, centers):
    unit_rows = unit_norm(samples)
    unit_centers = unit_norm(centers)
    affinity_scores = lax.dot_general(unit_rows, unit_centers, (((1,), (1,)), ((), ())), preferred_element_type=jnp.float32)
    kmeans_kernel = jnp.exp(affinity_scores / SOFTMAX_TEMP_VALUE)
    row_scaling_factor = jnp.ones((NROWS,), jnp.float32)
    list_scale = jnp.ones((KLISTS,), jnp.float32)
    for step in range(ITERS):
        column_total = lax.optimization_barrier(jnp.sum(row_scaling_factor[:, None] * kmeans_kernel, 0))
        list_scale = 1.0 / (KLISTS * column_total)
        row_total = lax.optimization_barrier(jnp.sum(kmeans_kernel * list_scale[None, :], 1))
        row_scaling_factor = 1.0 / (NROWS * row_total)
    assignment = (NROWS * row_scaling_factor[:, None] * kmeans_kernel * list_scale[None, :]).astype(jnp.bfloat16)
    list_mass = lax.optimization_barrier(jnp.sum(assignment.astype(jnp.float32), 0))
    weighted_sum = lax.dot_general(assignment, unit_rows, (((0,), (0,)), ((), ())), preferred_element_type=jnp.float32)
    new_centers = square_root_math(D) * weighted_sum / list_mass[:, None]
    return (assignment, new_centers)

def square_root_math(value):
    return jnp.sqrt(jnp.float32(value))
```

```python
import functools

import jax
import jax.numpy as jnp
from jax import lax
from jax.experimental import pallas as pl
from jax.experimental.pallas import tpu as pltpu
from jax.sharding import PartitionSpec as P

ITERS = 3
SOFTMAX_TEMP_VALUE = 0.03
EXP2_SCALE = 1.0 / (SOFTMAX_TEMP_VALUE * 0.6931471805599453)
F32 = jnp.float32
BF16 = jnp.bfloat16
MESH = pl.DeviceIdType.MESH
NT = (((1,), (1,)), ((), ()))
LANES = 128


def unit_norm(block):
    wide = block.astype(F32)
    scale = 1.0 / jnp.sqrt(jnp.sum(wide * wide, 1, keepdims=True) + 1e-06)
    return (wide * scale).astype(BF16)


def affinity(left, right):
    scores = lax.dot_general(left, right, NT, preferred_element_type=F32)
    return jnp.exp2(scores * EXP2_SCALE)


def hops(step, size):
    return min(step, size - step)


def kernel(
    ny, nx, nz, total_rows, total_lists,
    samples, centers, out, new_centers,
    uall, cn, km, ko, kt, ut, stage, lhs, lhs_w, rcol,
    msg_c, msg_r, slots_c, slots_r, part_msg, part_in, list_in, list_own,
    w_out, w_in, row_out,
    ssem_c, rsem_c, ssem_r, rsem_r, sib_s, sib_r, ssem_w, rsem_w, out_sem,
):
    rows = samples.shape[0]
    half = centers.shape[0] // 2
    chip_rows = 2 * rows
    width = samples.shape[1]
    chips = ny * nx

    place = lax.axis_index("rows")
    z = lax.axis_index("lists")
    y = place // (2 * nx)
    x = (place // 2) % nx
    c = place % 2
    other = 1 - c

    def at(dy, dx, dc, dz):
        return (
            (((y + dy) % ny) * nx + (x + dx) % nx) * 2 + (c + dc) % 2,
            (z + dz) % nz,
        )

    sibling = at(0, 0, 1, 0)
    xy = [(dy, dx) for dy in range(ny) for dx in range(nx) if (dy, dx) != (0, 0)]
    xy.sort(key=lambda o: -(hops(o[0], ny) + hops(o[1], nx)))
    zc = [(dz, dc) for dz in range(nz) for dc in range(2) if (dz, dc) != (0, 0)]
    zc.sort(key=lambda o: -hops(o[0], nz))

    barrier = pltpu.get_barrier_semaphore()
    for dy, dx in xy:
        pl.semaphore_signal(barrier, inc=1, device_id=at(dy, dx, 0, 0), device_id_type=MESH)
    for dz, dc in zc:
        pl.semaphore_signal(barrier, inc=1, device_id=at(0, 0, dc, dz), device_id_type=MESH)

    own_rows = pl.ds(pl.multiple_of(c * rows, rows), rows)
    sib_rows = pl.ds(pl.multiple_of(other * rows, rows), rows)

    def norm_centers(which, parity):
        def step(j, _):
            src = pl.ds(pl.multiple_of((2 * j + parity) * LANES, LANES), LANES)
            dst = pl.ds(pl.multiple_of(j * LANES, LANES), LANES)
            cn[which, dst, :] = unit_norm(centers[src, :])
            return 0

        lax.fori_loop(0, half // LANES, step, 0)

    def to_rows(dst, vec):
        for i in range(dst.shape[0]):
            dst[i : i + 1, :] = vec[:, i * LANES : (i + 1) * LANES]

    def split_lhs(compact):
        high = compact.astype(BF16).astype(F32)
        low = compact - high
        for i in range(compact.shape[0]):
            lhs[0:1, i * LANES : (i + 1) * LANES] = high[i : i + 1, :]
            lhs[1:2, i * LANES : (i + 1) * LANES] = low[i : i + 1, :]

    def matvec(count, mat):
        got = jnp.dot(lhs[:, :count].astype(BF16), mat[...], preferred_element_type=F32)
        return got[0:1, :] + got[1:2, :]

    def exchange_start(msg, slots, ssem, rsem, targets):
        for slot, target in targets:
            pltpu.make_async_remote_copy(
                src_ref=msg, dst_ref=slots.at[slot], send_sem=ssem, recv_sem=rsem,
                device_id=target, device_id_type=MESH,
            ).start()

    def exchange_sum(msg, slots, rsem, count):
        arrived = slots.at[pl.ds(1, count - 1)]
        pltpu.make_async_copy(arrived, arrived, rsem).wait()
        total = msg[...]
        for i in range(1, count):
            total = total + slots[i]
        return total

    def sent(slots, ssem, count):
        gone = slots.at[pl.ds(1, count - 1)]
        pltpu.make_async_copy(gone, gone, ssem).wait()

    targets_c = [(dy * nx + dx, at(dy, dx, 0, 0)) for dy, dx in xy]
    targets_r = [(dz * 2 + dc, at(0, 0, dc, dz)) for dz, dc in zc]

    lhs[...] = jnp.zeros_like(lhs)
    uall[own_rows, :] = unit_norm(samples[...])
    norm_centers(1, other)
    block = affinity(uall[own_rows, :], cn[1])
    ko[...] = block.astype(BF16)
    to_rows(part_msg, jnp.sum(block, 0, keepdims=True))
    pl.semaphore_wait(barrier, len(xy) + len(zc))
    send_part = pltpu.make_async_remote_copy(
        src_ref=part_msg, dst_ref=part_in, send_sem=sib_s.at[0], recv_sem=sib_r.at[0],
        device_id=sibling, device_id_type=MESH,
    )
    send_part.start()
    send_rows = pltpu.make_async_remote_copy(
        src_ref=uall.at[own_rows], dst_ref=uall.at[own_rows],
        send_sem=sib_s.at[1], recv_sem=sib_r.at[1],
        device_id=sibling, device_id_type=MESH,
    )
    send_rows.start()
    norm_centers(0, c)
    block = affinity(uall[own_rows, :], cn[0])
    km[own_rows, :] = block.astype(BF16)
    to_rows(msg_c.at[0], jnp.sum(block, 0, keepdims=True))
    send_part.wait()
    msg_c[0] = msg_c[0] + part_in[...]

    send_lists = None
    row_scale = None
    list_scale = None
    for it in range(ITERS):
        if it > 0:
            split_lhs(row_scale)
            to_rows(msg_c.at[it], matvec(chip_rows, km))
        exchange_start(msg_c.at[it], slots_c.at[it], ssem_c.at[it], rsem_c.at[it], targets_c)
        if it == 0:
            kt[:, own_rows] = affinity(cn[0], uall[own_rows, :]).astype(BF16)
            send_rows.wait()
            kt[:, sib_rows] = affinity(cn[0], uall[sib_rows, :]).astype(BF16)
        column_total = exchange_sum(msg_c.at[it], slots_c.at[it], rsem_c.at[it], chips)
        list_scale = 1.0 / (total_lists * column_total)
        if it == ITERS - 1:
            list_own[...] = list_scale
            send_lists = pltpu.make_async_remote_copy(
                src_ref=list_own, dst_ref=list_in, send_sem=sib_s.at[2], recv_sem=sib_r.at[2],
                device_id=sibling, device_id_type=MESH,
            )
            send_lists.start()
        split_lhs(list_scale)
        to_rows(msg_r.at[it], matvec(half, kt))
        exchange_start(msg_r.at[it], slots_r.at[it], ssem_r.at[it], rsem_r.at[it], targets_r)
        if it == 0:
            km[sib_rows, :] = affinity(uall[sib_rows, :], cn[0]).astype(BF16)
            ut[...] = uall[...].astype(F32).T
        row_total = exchange_sum(msg_r.at[it], slots_r.at[it], rsem_r.at[it], 2 * nz)
        row_scale = 1.0 / (total_rows * row_total)

    for i in range(chip_rows // LANES):
        lanes = pl.ds(i * LANES, LANES)
        one = row_scale[i : i + 1, :]
        lhs_w[0:width, lanes] = (ut[:, lanes] * one).astype(BF16)
        high = one.astype(BF16).astype(F32)
        index = lax.broadcasted_iota(jnp.int32, (16, LANES), 0)
        lhs_w[width : width + 16, lanes] = jnp.where(
            index == 0, high, jnp.where(index == 1, one - high, 0.0)
        ).astype(BF16)

    order = [(dy, dx) for dy, dx in xy] + [(0, 0)]
    for g in range(0, chips, 4):
        group = order[g : g + 4]
        blocks = []
        for dy, dx in group:
            dest = ((y + dy) % ny) * nx + (x + dx) % nx
            blocks.append(km[:, pl.ds(pl.multiple_of(dest * LANES, LANES), LANES)])
        got = jnp.dot(
            lhs_w[...], jnp.concatenate(blocks, 1), preferred_element_type=F32
        )
        for n, (dy, dx) in enumerate(group):
            slot = dy * nx + dx
            piece = got[:, n * LANES : (n + 1) * LANES]
            mass = piece[width : width + 1] + piece[width + 1 : width + 2]
            high = mass.astype(BF16).astype(F32)
            mid = (mass - high).astype(BF16).astype(F32)
            index = lax.broadcasted_iota(jnp.int32, (16, LANES), 0)
            tail = jnp.where(
                index == 0, high,
                jnp.where(index == 1, mid, jnp.where(index == 2, mass - high - mid, 0.0)),
            )
            dst = w_in if slot == 0 else w_out
            dst[slot, 0:width, :] = piece[0:width].astype(BF16)
            dst[slot, width : width + 16, :] = tail.astype(BF16)
            if slot != 0:
                pltpu.make_async_remote_copy(
                    src_ref=w_out.at[slot], dst_ref=w_in.at[slot],
                    send_sem=ssem_w, recv_sem=rsem_w,
                    device_id=at(dy, dx, 0, 0), device_id_type=MESH,
                ).start()

    row_out[...] = total_rows * row_scale
    first = c * (rows // LANES)
    for i in range(rows // LANES):
        line = row_out[pl.ds(first + i, 1), :]
        rcol[i * LANES : (i + 1) * LANES, :] = jnp.broadcast_to(line, (LANES, LANES)).T
    send_lists.wait()

    def assign(i, _):
        block_rows = pl.ds(pl.multiple_of(i * LANES, LANES), LANES)
        main_rows = pl.ds(pl.multiple_of(c * rows + i * LANES, LANES), LANES)

        def inner(q, _):
            at_rows = pl.ds(pl.multiple_of(i * LANES + q * 16, 16), 16)
            at_main = pl.ds(pl.multiple_of(c * rows + i * LANES + q * 16, 16), 16)
            scale = rcol[at_rows, :]
            for j in range(half // LANES):
                lanes = pl.ds(j * LANES, LANES)
                one = km[at_main, lanes].astype(F32) * scale * list_own[j : j + 1, :]
                two = ko[at_rows, lanes].astype(F32) * scale * list_in[j : j + 1, :]
                stage[at_rows, pl.ds(pl.multiple_of((2 * j + c) * LANES, LANES), LANES)] = (
                    one.astype(BF16)
                )
                stage[at_rows, pl.ds(pl.multiple_of((2 * j + other) * LANES, LANES), LANES)] = (
                    two.astype(BF16)
                )
            return 0

        lax.fori_loop(0, LANES // 16, inner, 0)
        pltpu.make_async_copy(stage.at[block_rows], out.at[block_rows], out_sem).start()
        return 0

    lax.fori_loop(0, rows // LANES, assign, 0)

    arrived = w_in.at[pl.ds(1, chips - 1)]
    pltpu.make_async_copy(arrived, arrived, rsem_w).wait()
    total = w_in[0].astype(F32)
    for i in range(1, chips):
        total = total + w_in[i].astype(F32)
    mass = total[width : width + 1] + total[width + 1 : width + 2] + total[width + 2 : width + 3]
    new_centers[...] = (jnp.sqrt(F32(width)) * total[0:width] / mass).T

    sent(w_in, ssem_w, chips)
    for it in range(ITERS):
        sent(slots_c.at[it], ssem_c.at[it], chips)
        sent(slots_r.at[it], ssem_r.at[it], 2 * nz)
    pltpu.make_async_copy(stage, out, out_sem).wait()


def solution(mesh):
    row_devices = mesh.shape["rows"]
    nz = mesh.shape["lists"]
    ny = nx = round((row_devices // 2) ** 0.5)

    def body(samples, centers):
        rows, width = samples.shape
        lists = centers.shape[0]
        half, chip_rows, chips = lists // 2, 2 * rows, ny * nx
        mc, mr = half // LANES, chip_rows // LANES
        dma = pltpu.SemaphoreType.DMA
        vmem = pl.BlockSpec(memory_space=pltpu.VMEM)
        return pl.pallas_call(
            functools.partial(
                kernel, ny, nx, nz, float(rows * row_devices), float(lists * nz)
            ),
            out_shape=(
                jax.ShapeDtypeStruct((rows, lists), BF16),
                jax.ShapeDtypeStruct((lists // row_devices, width), F32),
            ),
            in_specs=[vmem, vmem],
            out_specs=(pl.BlockSpec(memory_space=pl.ANY), vmem),
            scratch_shapes=[
                pltpu.VMEM((chip_rows, width), BF16),
                pltpu.VMEM((2, half, width), BF16),
                pltpu.VMEM((chip_rows, half), BF16),
                pltpu.VMEM((rows, half), BF16),
                pltpu.VMEM((half, chip_rows), BF16),
                pltpu.VMEM((width, chip_rows), F32),
                pltpu.VMEM((rows, lists), BF16),
                pltpu.VMEM((16, max(half, chip_rows)), F32),
                pltpu.VMEM((width + 16, chip_rows), BF16),
                pltpu.VMEM((rows, LANES), F32),
                pltpu.VMEM((ITERS, mc, LANES), F32),
                pltpu.VMEM((ITERS, mr, LANES), F32),
                pltpu.VMEM((ITERS, chips, mc, LANES), F32),
                pltpu.VMEM((ITERS, 2 * nz, mr, LANES), F32),
                pltpu.VMEM((mc, LANES), F32),
                pltpu.VMEM((mc, LANES), F32),
                pltpu.VMEM((mc, LANES), F32),
                pltpu.VMEM((mc, LANES), F32),
                pltpu.VMEM((chips, width + 16, LANES), BF16),
                pltpu.VMEM((chips, width + 16, LANES), BF16),
                pltpu.VMEM((mr, LANES), F32),
                dma((ITERS,)),
                dma((ITERS,)),
                dma((ITERS,)),
                dma((ITERS,)),
                dma((3,)),
                dma((3,)),
                dma,
                dma,
                dma,
            ],
            compiler_params=pltpu.CompilerParams(
                collective_id=0, has_side_effects=True, vmem_limit_bytes=60 * 2**20
            ),
        )(samples, centers)

    return jax.shard_map(
        body,
        mesh=mesh,
        in_specs=(P("rows", None), P("lists", None)),
        out_specs=(P("rows", "lists"), P(("lists", "rows"), None)),
        check_vma=False,
    )
```

```python
import functools

import jax
import jax.numpy as jnp
from jax import lax
from jax.experimental import pallas as pl
from jax.experimental.pallas import tpu as pltpu
from jax.sharding import PartitionSpec as P

ITERS = 3
SOFTMAX_TEMP_VALUE = 0.03
EXP2_SCALE = 1.0 / (SOFTMAX_TEMP_VALUE * 0.6931471805599453)
F32 = jnp.float32
BF16 = jnp.bfloat16
MESH = pl.DeviceIdType.MESH
NT = (((1,), (1,)), ((), ()))
LANES = 128


def unit_norm(block):
    wide = block.astype(F32)
    scale = 1.0 / jnp.sqrt(jnp.sum(wide * wide, 1, keepdims=True) + 1e-06)
    return (wide * scale).astype(BF16)


def affinity(left, right):
    scores = lax.dot_general(left, right, NT, preferred_element_type=F32)
    return jnp.exp2(scores * EXP2_SCALE)


def hops(step, size):
    return min(step, size - step)


def mass_rows(mass):
    high = mass.astype(BF16).astype(F32)
    mid = (mass - high).astype(BF16).astype(F32)
    index = lax.broadcasted_iota(jnp.int32, (16, LANES), 0)
    return jnp.where(
        index == 0, high,
        jnp.where(index == 1, mid, jnp.where(index == 2, mass - high - mid, 0.0)),
    ).astype(BF16)


def mass_of(tail):
    return tail[0:1] + tail[1:2] + tail[2:3]


def kernel(
    ny, nx, nz, total_rows, total_lists,
    samples, centers, out, new_centers,
    xs, cs, uall, cn, km, ko, kt, ut, lhs_w, rcol, sums,
    own_c, msg_c, slots_c, own_r, msg_r, slots_r, part_msg, part_in, list_own, list_in,
    w_out, wa1, wb1, wa2_out, wb2_out, wa2, wb2,
    in_sem, ssem_c, rsem_c, ssem_r, rsem_r, sib_s, sib_r,
    ss_a1, rs_a1, ss_b1, rs_b1, ss_2, rs_2,
):
    rows, width = xs.shape
    half = cs.shape[1] * LANES
    chip_rows = 2 * rows
    chips = ny * nx
    front = width // 2 + 16

    place = lax.axis_index("rows")
    z = lax.axis_index("lists")
    y = place // (2 * nx)
    x = (place // 2) % nx
    c = place % 2
    other = 1 - c

    def at(dy, dx, dc, dz):
        return (
            (((y + dy) % ny) * nx + (x + dx) % nx) * 2 + (c + dc) % 2,
            (z + dz) % nz,
        )

    def remote(src, dst, ssem, rsem, target):
        return pltpu.make_async_remote_copy(
            src_ref=src, dst_ref=dst, send_sem=ssem, recv_sem=rsem,
            device_id=target, device_id_type=MESH,
        )

    def settle(ref, sem):
        pltpu.make_async_copy(ref, ref, sem).wait()

    sibling = at(0, 0, 1, 0)
    xy = [(dy, dx) for dy in range(ny) for dx in range(nx) if (dy, dx) != (0, 0)]
    xy.sort(key=lambda o: -(hops(o[0], ny) + hops(o[1], nx)))
    zc = [(dz, dc) for dz in range(nz) for dc in range(2) if (dz, dc) != (0, 0)]
    zc.sort(key=lambda o: -hops(o[0], nz))

    barrier = pltpu.get_barrier_semaphore()
    for dy, dx in xy:
        pl.semaphore_signal(barrier, inc=1, device_id=at(dy, dx, 0, 0), device_id_type=MESH)
    for dz, dc in zc:
        pl.semaphore_signal(barrier, inc=1, device_id=at(0, 0, dc, dz), device_id_type=MESH)

    loads = [
        pltpu.make_async_copy(samples, xs, in_sem.at[0]),
        pltpu.make_async_copy(centers.at[:, other], cs.at[1], in_sem.at[1]),
        pltpu.make_async_copy(centers.at[:, c], cs.at[0], in_sem.at[2]),
    ]
    for load in loads:
        load.start()

    own_rows = pl.ds(pl.multiple_of(c * rows, rows), rows)
    sib_rows = pl.ds(pl.multiple_of(other * rows, rows), rows)

    def to_rows(dst, vec):
        for i in range(dst.shape[0]):
            dst[i : i + 1, :] = vec[:, i * LANES : (i + 1) * LANES]

    def spread(compact):
        for i in range(compact.shape[0]):
            rcol[i * LANES : (i + 1) * LANES, :] = jnp.broadcast_to(
                compact[i : i + 1, :], (LANES, LANES)
            ).T

    def contract(compact, mat, dst):
        spread(compact)
        depth, count = mat.shape
        total = None
        for i in range(0, depth, LANES):
            scale = jnp.concatenate([rcol[i : i + LANES, :]] * (count // LANES), 1)
            term = mat[i : i + LANES, :].astype(F32) * scale
            term = jnp.sum(term.reshape(LANES // 8, 8, count), 0)
            total = term if total is None else total + term
        for i in range(count // LANES):
            dst[i : i + 1, :] = jnp.sum(total[:, i * LANES : (i + 1) * LANES], 0, keepdims=True)

    def exchange_start(own, msg, slots, ssem, rsem, targets):
        msg[...] = own[...].astype(BF16)
        for slot, target in targets:
            remote(msg, slots.at[slot], ssem, rsem, target).start()

    def exchange_sum(own, slots, rsem, count):
        settle(slots.at[pl.ds(1, count - 1)], rsem)
        total = own[...]
        for i in range(1, count):
            total = total + slots[i].astype(F32)
        return total

    targets_c = [(dy * nx + dx, at(dy, dx, 0, 0)) for dy, dx in xy]
    targets_r = [(dz * 2 + dc, at(0, 0, dc, dz)) for dz, dc in zc]

    loads[0].wait()
    uall[own_rows, :] = unit_norm(xs[...])
    loads[1].wait()
    cn[1] = unit_norm(cs[1].reshape(half, width))
    block = affinity(uall[own_rows, :], cn[1])
    ko[...] = block.astype(BF16)
    to_rows(part_msg, jnp.sum(block, 0, keepdims=True))
    pl.semaphore_wait(barrier, len(xy) + len(zc))
    send_part = remote(part_msg, part_in, sib_s.at[0], sib_r.at[0], sibling)
    send_part.start()
    send_rows = remote(
        uall.at[own_rows], uall.at[own_rows], sib_s.at[1], sib_r.at[1], sibling
    )
    send_rows.start()
    loads[2].wait()
    cn[0] = unit_norm(cs[0].reshape(half, width))
    block = affinity(uall[own_rows, :], cn[0])
    km[own_rows, :] = block.astype(BF16)
    to_rows(sums, jnp.sum(block, 0, keepdims=True))
    send_part.wait()
    own_c[0] = sums[...] + part_in[...]

    send_lists = None
    row_scale = None
    for it in range(ITERS):
        if it > 0:
            contract(row_scale, km, own_c.at[it])
        exchange_start(
            own_c.at[it], msg_c.at[it], slots_c.at[it], ssem_c.at[it], rsem_c.at[it], targets_c
        )
        if it == 0:
            kt[:, own_rows] = affinity(cn[0], uall[own_rows, :]).astype(BF16)
            send_rows.wait()
            kt[:, sib_rows] = affinity(cn[0], uall[sib_rows, :]).astype(BF16)
        column_total = exchange_sum(own_c.at[it], slots_c.at[it], rsem_c.at[it], chips)
        list_scale = 1.0 / (total_lists * column_total)
        if it == ITERS - 1:
            list_own[...] = list_scale
            send_lists = remote(list_own, list_in, sib_s.at[2], sib_r.at[2], sibling)
            send_lists.start()
        contract(list_scale, kt, own_r.at[it])
        exchange_start(
            own_r.at[it], msg_r.at[it], slots_r.at[it], ssem_r.at[it], rsem_r.at[it], targets_r
        )
        if it == 0:
            km[sib_rows, :] = affinity(uall[sib_rows, :], cn[0]).astype(BF16)
            ut[...] = uall[...].astype(F32).T
        row_total = exchange_sum(own_r.at[it], slots_r.at[it], rsem_r.at[it], 2 * nz)
        row_scale = 1.0 / (total_rows * row_total)

    index = lax.broadcasted_iota(jnp.int32, (16, LANES), 0)
    for i in range(chip_rows // LANES):
        lanes = pl.ds(i * LANES, LANES)
        one = row_scale[i : i + 1, :]
        lhs_w[0:width, lanes] = (ut[:, lanes] * one).astype(BF16)
        high = one.astype(BF16).astype(F32)
        lhs_w[width : width + 16, lanes] = jnp.where(
            index == 0, high, jnp.where(index == 1, one - high, 0.0)
        ).astype(BF16)

    def reach(o):
        a, b = hops(o[0], ny), hops(o[1], nx)
        return -(4 * max(a, b) + a + b)

    order = sorted(xy + [(0, 0)], key=reach)
    for g in range(0, chips, 4):
        group = order[g : g + 4]
        blocks = []
        for dy, dx in group:
            dest = ((y + dy) % ny) * nx + (x + dx) % nx
            blocks.append(km[:, pl.ds(pl.multiple_of(dest * LANES, LANES), LANES)])
        got = jnp.dot(
            lhs_w[...], jnp.concatenate(blocks, 1), preferred_element_type=F32
        )
        for n, (dy, dx) in enumerate(group):
            slot = dy * nx + dx
            piece = got[:, n * LANES : (n + 1) * LANES]
            mass = piece[width : width + 1] + piece[width + 1 : width + 2]
            first = wa1.at[dy, 0] if dx == 0 else w_out.at[slot, pl.ds(0, front)]
            second = wb1.at[dx, 0] if dy == 0 else w_out.at[slot, pl.ds(front, width // 2)]
            first[0 : width // 2, :] = piece[0 : width // 2].astype(BF16)
            first[width // 2 : front, :] = mass_rows(mass)
            second[...] = piece[width // 2 : width].astype(BF16)
            if dx != 0:
                remote(first, wa1.at[dy, dx], ss_a1.at[dy], rs_a1.at[dy], at(0, dx, 0, 0)).start()
            if dy != 0:
                remote(second, wb1.at[dx, dy], ss_b1.at[dx], rs_b1.at[dx], at(dy, 0, 0, 0)).start()

    final_rows = total_rows * row_scale
    spread(final_rows)
    send_lists.wait()

    def assign(start, stop):
        for parity in range(2):
            @pl.when(c == parity)
            def _():
                def step(i, _):
                    here = pl.ds(pl.multiple_of(i * 16, 16), 16)
                    there = pl.ds(pl.multiple_of(parity * rows + i * 16, 16), 16)
                    scale = rcol[there, :]
                    for j in range(half // LANES):
                        lanes = pl.ds(j * LANES, LANES)
                        one = km[there, lanes].astype(F32) * scale * list_own[j : j + 1, :]
                        two = ko[here, lanes].astype(F32) * scale * list_in[j : j + 1, :]
                        out[here, pl.ds((2 * j + parity) * LANES, LANES)] = one.astype(BF16)
                        out[here, pl.ds((2 * j + 1 - parity) * LANES, LANES)] = two.astype(BF16)
                    return 0

                lax.fori_loop(start, stop, step, 0)

    steps = rows // 16
    assign(0, steps // 2)

    def gather(slots, count):
        total = slots[0].astype(F32)
        for i in range(1, count):
            total = total + slots[i].astype(F32)
        return total

    def stage_a(dy):
        settle(wa1.at[dy, pl.ds(1, nx - 1)], rs_a1.at[dy])
        return gather(wa1.at[dy], nx)

    def stage_b(dx):
        settle(wb1.at[dx, pl.ds(1, ny - 1)], rs_b1.at[dx])
        return gather(wb1.at[dx], ny)

    for step in sorted(range(1, ny), key=lambda o: -hops(o, ny)):
        total = stage_a(step)
        wa2_out[step, 0 : width // 2, :] = total[0 : width // 2].astype(BF16)
        wa2_out[step, width // 2 : front, :] = mass_rows(mass_of(total[width // 2 : front]))
        remote(wa2_out.at[step], wa2.at[step], ss_2.at[0], rs_2.at[0], at(step, 0, 0, 0)).start()
        total = stage_b(step)
        wb2_out[step] = total.astype(BF16)
        remote(wb2_out.at[step], wb2.at[step], ss_2.at[1], rs_2.at[1], at(0, step, 0, 0)).start()

    assign(steps // 2, steps)

    first = stage_a(0)
    second = stage_b(0)
    settle(wa2.at[pl.ds(1, ny - 1)], rs_2.at[0])
    for i in range(1, ny):
        first = first + wa2[i].astype(F32)
    settle(wb2.at[pl.ds(1, nx - 1)], rs_2.at[1])
    for i in range(1, nx):
        second = second + wb2[i].astype(F32)
    scale = jnp.sqrt(F32(width)) / mass_of(first[width // 2 : front])
    new_centers[:, 0 : width // 2] = (first[0 : width // 2] * scale).T
    new_centers[:, width // 2 : width] = (second * scale).T

    for i in range(ny):
        settle(wa1.at[i, pl.ds(1, nx - 1)], ss_a1.at[i])
    for i in range(nx):
        settle(wb1.at[i, pl.ds(1, ny - 1)], ss_b1.at[i])
    settle(wa2.at[pl.ds(1, ny - 1)], ss_2.at[0])
    settle(wb2.at[pl.ds(1, nx - 1)], ss_2.at[1])
    for it in range(ITERS):
        settle(slots_c.at[it, pl.ds(1, chips - 1)], ssem_c.at[it])
        settle(slots_r.at[it, pl.ds(1, 2 * nz - 1)], ssem_r.at[it])


def write_out(assignment, new_centers, out, out_centers, sems):
    pieces = 8
    size = assignment.shape[0] // pieces
    copies = [
        pltpu.make_async_copy(
            assignment.at[pl.ds(i * size, size)], out.at[pl.ds(i * size, size)], sems.at[i]
        )
        for i in range(pieces)
    ]
    copies.append(pltpu.make_async_copy(new_centers, out_centers, sems.at[pieces]))
    for copy in copies:
        copy.start()
    for copy in copies:
        copy.wait()


def solution(mesh):
    row_devices = mesh.shape["rows"]
    nz = mesh.shape["lists"]
    ny = nx = round((row_devices // 2) ** 0.5)

    def body(samples, centers):
        rows, width = samples.shape
        lists = centers.shape[0]
        half, chip_rows, chips = lists // 2, 2 * rows, ny * nx
        mc, mr = half // LANES, chip_rows // LANES
        front = width // 2 + 16
        dma = pltpu.SemaphoreType.DMA
        vmem = pl.BlockSpec(memory_space=pltpu.VMEM)
        hbm = pl.BlockSpec(memory_space=pl.ANY)
        big = ((rows, lists), BF16)
        small = ((lists // row_devices, width), F32)
        assignment, new_centers = pl.pallas_call(
            functools.partial(
                kernel, ny, nx, nz, float(rows * row_devices), float(lists * nz)
            ),
            out_shape=(pltpu.VMEM(*big), pltpu.VMEM(*small)),
            in_specs=[hbm, hbm],
            out_specs=(vmem, vmem),
            scratch_shapes=[
                pltpu.VMEM((rows, width), BF16),
                pltpu.VMEM((2, half // LANES, LANES, width), BF16),
                pltpu.VMEM((chip_rows, width), BF16),
                pltpu.VMEM((2, half, width), BF16),
                pltpu.VMEM((chip_rows, half), BF16),
                pltpu.VMEM((rows, half), BF16),
                pltpu.VMEM((half, chip_rows), BF16),
                pltpu.VMEM((width, chip_rows), F32),
                pltpu.VMEM((width + 16, chip_rows), BF16),
                pltpu.VMEM((max(half, chip_rows), LANES), F32),
                pltpu.VMEM((mc, LANES), F32),
                pltpu.VMEM((ITERS, mc, LANES), F32),
                pltpu.VMEM((ITERS, mc, LANES), BF16),
                pltpu.VMEM((ITERS, chips, mc, LANES), BF16),
                pltpu.VMEM((ITERS, mr, LANES), F32),
                pltpu.VMEM((ITERS, mr, LANES), BF16),
                pltpu.VMEM((ITERS, 2 * nz, mr, LANES), BF16),
                pltpu.VMEM((mc, LANES), F32),
                pltpu.VMEM((mc, LANES), F32),
                pltpu.VMEM((mc, LANES), F32),
                pltpu.VMEM((mc, LANES), F32),
                pltpu.VMEM((chips, width + 16, LANES), BF16),
                pltpu.VMEM((ny, nx, front, LANES), BF16),
                pltpu.VMEM((nx, ny, width // 2, LANES), BF16),
                pltpu.VMEM((ny, front, LANES), BF16),
                pltpu.VMEM((nx, width // 2, LANES), BF16),
                pltpu.VMEM((ny, front, LANES), BF16),
                pltpu.VMEM((nx, width // 2, LANES), BF16),
                dma((3,)),
                dma((ITERS,)),
                dma((ITERS,)),
                dma((ITERS,)),
                dma((ITERS,)),
                dma((3,)),
                dma((3,)),
                dma((ny,)),
                dma((ny,)),
                dma((nx,)),
                dma((nx,)),
                dma((2,)),
                dma((2,)),
            ],
            compiler_params=pltpu.CompilerParams(
                collective_id=0, has_side_effects=True, vmem_limit_bytes=50 * 2**20
            ),
        )(samples, centers.reshape(half // LANES, 2, LANES, width))
        return tuple(
            pl.pallas_call(
                write_out,
                out_shape=(jax.ShapeDtypeStruct(*big), jax.ShapeDtypeStruct(*small)),
                in_specs=[vmem, vmem],
                out_specs=(hbm, hbm),
                scratch_shapes=[dma((9,))],
                compiler_params=pltpu.CompilerParams(vmem_limit_bytes=2**20),
            )(
                pltpu.with_memory_space_constraint(assignment, pltpu.VMEM),
                pltpu.with_memory_space_constraint(new_centers, pltpu.VMEM),
            )
        )

    return jax.shard_map(
        body,
        mesh=mesh,
        in_specs=(P("rows", None), P("lists", None)),
        out_specs=(P("rows", "lists"), P(("lists", "rows"), None)),
        check_vma=False,
    )
```

```python
import functools

import jax
import jax.numpy as jnp
from jax import lax
from jax.experimental import pallas as pl
from jax.experimental.pallas import tpu as pltpu
from jax.sharding import PartitionSpec as P

ITERS = 3
SOFTMAX_TEMP_VALUE = 0.03
EXP2_SCALE = 1.0 / (SOFTMAX_TEMP_VALUE * 0.6931471805599453)
F32 = jnp.float32
BF16 = jnp.bfloat16
MESH = pl.DeviceIdType.MESH
NT = (((1,), (1,)), ((), ()))
LANES = 128


def unit_norm(block):
    wide = block.astype(F32)
    return (wide * lax.rsqrt(jnp.sum(wide * wide, 1, keepdims=True) + 1e-06)).astype(BF16)


def affinity(left, right):
    scores = lax.dot_general(left, right, NT, preferred_element_type=F32)
    return jnp.exp2(scores * EXP2_SCALE)


def hops(step, size):
    return min(step, size - step)


def kernel(
    ny, nx, nz, total_rows, total_lists,
    samples, centers, out, raw,
    xs, cs, uall, cn, km, ko, kt, ut, lhs_w, rcol, sums,
    msg_0, slots_0, own_c, msg_c, slots_c, own_r, msg_r, slots_r, list_own, list_in,
    mass_out, mass_in, w_out, wa1, wb1, wa2_out, wb2_out, wa2, wb2,
    in_sem, sem_0, ssem_c, rsem_c, ssem_r, rsem_r, sib_s, sib_r, sem_m,
    ss_a1, rs_a1, ss_b1, rs_b1, ss_2, rs_2,
):
    rows, width = xs.shape
    half = cs.shape[1] * LANES
    chip_rows = 2 * rows
    chips = ny * nx
    part = width // 2

    place = lax.axis_index("rows")
    z = lax.axis_index("lists")
    y = place // (2 * nx)
    x = (place // 2) % nx
    c = place % 2
    other = 1 - c

    def at(dy, dx, dc, dz):
        return (
            (((y + dy) % ny) * nx + (x + dx) % nx) * 2 + (c + dc) % 2,
            (z + dz) % nz,
        )

    def remote(src, dst, ssem, rsem, target):
        return pltpu.make_async_remote_copy(
            src_ref=src, dst_ref=dst, send_sem=ssem, recv_sem=rsem,
            device_id=target, device_id_type=MESH,
        )

    def settle(ref, sem):
        pltpu.make_async_copy(ref, ref, sem).wait()

    sibling = at(0, 0, 1, 0)
    xy = [(dy, dx) for dy in range(ny) for dx in range(nx) if (dy, dx) != (0, 0)]
    xy.sort(key=lambda o: -(hops(o[0], ny) + hops(o[1], nx)))
    zc = [(dz, dc) for dz in range(nz) for dc in range(2) if (dz, dc) != (0, 0)]
    zc.sort(key=lambda o: -hops(o[0], nz))
    xyc = [(dy, dx, dc) for dy, dx in xy for dc in range(2)] + [(0, 0, 1)]

    loads = [
        pltpu.make_async_copy(samples, xs, in_sem.at[0]),
        pltpu.make_async_copy(centers.at[:, other], cs.at[1], in_sem.at[1]),
        pltpu.make_async_copy(centers.at[:, c], cs.at[0], in_sem.at[2]),
    ]
    for load in loads:
        load.start()

    barrier = pltpu.get_barrier_semaphore()
    for dy, dx, dc in xyc:
        pl.semaphore_signal(barrier, inc=1, device_id=at(dy, dx, dc, 0), device_id_type=MESH)
    for dz, dc in zc:
        if dz != 0:
            pl.semaphore_signal(
                barrier, inc=1, device_id=at(0, 0, dc, dz), device_id_type=MESH
            )

    own_rows = pl.ds(pl.multiple_of(c * rows, rows), rows)
    sib_rows = pl.ds(pl.multiple_of(other * rows, rows), rows)

    def to_rows(dst, vec):
        for i in range(dst.shape[0]):
            dst[i : i + 1, :] = vec[:, i * LANES : (i + 1) * LANES]

    def spread(compact):
        for i in range(compact.shape[0]):
            rcol[i * LANES : (i + 1) * LANES, :] = jnp.broadcast_to(
                compact[i : i + 1, :], (LANES, LANES)
            ).T

    def contract(compact, mat, dst):
        count = compact.shape[0]
        high = compact.astype(BF16).astype(F32)
        low = compact - high
        terms = [
            jnp.concatenate([term[i : i + 1, :] for i in range(count)], 1)
            for term in (high, low)
        ]
        terms.append(jnp.zeros((14, count * LANES), F32))
        lhs = jnp.concatenate(terms, 0).astype(BF16)
        got = jnp.dot(lhs, mat[...], preferred_element_type=F32)
        to_rows(dst, got[0:1, :] + got[1:2, :])

    def exchange_start(own, msg, slots, ssem, rsem, targets):
        msg[...] = own[...].astype(BF16)
        for slot, target in targets:
            remote(msg, slots.at[slot], ssem, rsem, target).start()

    def exchange_sum(own, slots, rsem, count):
        settle(slots.at[pl.ds(1, count - 1)], rsem)
        total = own[...]
        for i in range(1, count):
            total = total + slots[i].astype(F32)
        return total

    targets_c = [(dy * nx + dx, at(dy, dx, 0, 0)) for dy, dx in xy]
    targets_r = [(dz * 2 + dc, at(0, 0, dc, dz)) for dz, dc in zc]

    loads[0].wait()
    uall[own_rows, :] = unit_norm(xs[...])
    for which in (1, 0):
        loads[2 - which].wait()
        cn[which] = unit_norm(cs[which].reshape(half, width))
        block = affinity(uall[own_rows, :], cn[which])
        if which == 1:
            ko[...] = block.astype(BF16)
        else:
            km[own_rows, :] = block.astype(BF16)
        to_rows(sums, jnp.sum(block, 0, keepdims=True))
        msg_0[which] = sums[...].astype(BF16)
    pl.semaphore_wait(barrier, len(xyc) + 2 * (nz - 1))
    for dy, dx, dc in xyc:
        remote(
            msg_0.at[dc], slots_0.at[(dy * nx + dx) * 2 + dc], sem_0.at[0], sem_0.at[1],
            at(dy, dx, dc, 0),
        ).start()
    send_rows = remote(
        uall.at[own_rows], uall.at[own_rows], sib_s.at[0], sib_r.at[0], sibling
    )
    send_rows.start()
    kt[:, own_rows] = affinity(cn[0], uall[own_rows, :]).astype(BF16)
    send_rows.wait()
    kt[:, sib_rows] = affinity(cn[0], uall[sib_rows, :]).astype(BF16)

    send_lists = None
    row_scale = None
    for it in range(ITERS):
        if it == 0:
            column_total = exchange_sum(sums, slots_0, sem_0.at[1], 2 * chips)
        else:
            own, slots = own_c.at[it - 1], slots_c.at[it - 1]
            contract(row_scale, km, own)
            exchange_start(
                own, msg_c.at[it - 1], slots, ssem_c.at[it - 1], rsem_c.at[it - 1], targets_c
            )
            column_total = exchange_sum(own, slots, rsem_c.at[it - 1], chips)
        list_scale = 1.0 / (total_lists * column_total)
        if it == ITERS - 1:
            list_own[...] = list_scale
            send_lists = remote(list_own, list_in, sib_s.at[1], sib_r.at[1], sibling)
            send_lists.start()
        contract(list_scale, kt, own_r.at[it])
        exchange_start(
            own_r.at[it], msg_r.at[it], slots_r.at[it], ssem_r.at[it], rsem_r.at[it], targets_r
        )
        if it == 0:
            km[sib_rows, :] = affinity(uall[sib_rows, :], cn[0]).astype(BF16)
            ut[...] = uall[...].astype(F32).T
        row_total = exchange_sum(own_r.at[it], slots_r.at[it], rsem_r.at[it], 2 * nz)
        row_scale = 1.0 / (total_rows * row_total)

    index = lax.broadcasted_iota(jnp.int32, (16, LANES), 0)
    for i in range(chip_rows // LANES):
        lanes = pl.ds(i * LANES, LANES)
        one = row_scale[i : i + 1, :]
        lhs_w[0:width, lanes] = (ut[:, lanes] * one).astype(BF16)
        high = one.astype(BF16).astype(F32)
        lhs_w[width : width + 16, lanes] = jnp.where(
            index == 0, high, jnp.where(index == 1, one - high, 0.0)
        ).astype(BF16)

    def reach(o):
        a, b = hops(o[0], ny), hops(o[1], nx)
        return (a * b == 0, -(4 * max(a, b) + a + b))

    order = sorted(xy + [(0, 0)], key=reach)
    cuts = [0] + list(range(2, chips, 4)) + [chips]
    for low, high in zip(cuts[:-1], cuts[1:]):
        group = order[low:high]
        blocks = []
        for dy, dx in group:
            dest = ((y + dy) % ny) * nx + (x + dx) % nx
            blocks.append(km[:, pl.ds(pl.multiple_of(dest * LANES, LANES), LANES)])
        got = jnp.dot(
            lhs_w[...], jnp.concatenate(blocks, 1), preferred_element_type=F32
        )
        for n, (dy, dx) in enumerate(group):
            slot = dy * nx + dx
            piece = got[:, n * LANES : (n + 1) * LANES]
            first = wa1.at[dy, 0] if dx == 0 else w_out.at[slot, pl.ds(0, part)]
            second = wb1.at[dx, 0] if dy == 0 else w_out.at[slot, pl.ds(part, part)]
            first[...] = piece[0:part].astype(BF16)
            second[...] = piece[part:width].astype(BF16)
            if dx != 0:
                remote(first, wa1.at[dy, dx], ss_a1.at[dy], rs_a1.at[dy], at(0, dx, 0, 0)).start()
            if dy != 0:
                remote(second, wb1.at[dx, dy], ss_b1.at[dx], rs_b1.at[dx], at(dy, 0, 0, 0)).start()
            mass = mass_in if slot == 0 else mass_out
            mass[slot] = piece[width : width + 1] + piece[width + 1 : width + 2]
            if slot != 0:
                remote(
                    mass_out.at[slot], mass_in.at[slot], sem_m.at[0], sem_m.at[1],
                    at(dy, dx, 0, 0),
                ).start()

    def assign():
        spread(total_rows * row_scale)
        send_lists.wait()
        for parity in range(2):
            @pl.when(c == parity)
            def _():
                def step(i, _):
                    here = pl.ds(pl.multiple_of(i * 16, 16), 16)
                    there = pl.ds(pl.multiple_of(parity * rows + i * 16, 16), 16)
                    scale = rcol[there, :]
                    for j in range(half // LANES):
                        lanes = pl.ds(j * LANES, LANES)
                        one = km[there, lanes].astype(F32) * scale * list_own[j : j + 1, :]
                        two = ko[here, lanes].astype(F32) * scale * list_in[j : j + 1, :]
                        out[here, pl.ds((2 * j + parity) * LANES, LANES)] = one.astype(BF16)
                        out[here, pl.ds((2 * j + 1 - parity) * LANES, LANES)] = two.astype(BF16)
                    return 0

                lax.fori_loop(0, rows // 16, step, 0)

    def gather(slots, count):
        total = slots[0].astype(F32)
        for i in range(1, count):
            total = total + slots[i].astype(F32)
        return total

    def stage_a(dy):
        settle(wa1.at[dy, pl.ds(1, nx - 1)], rs_a1.at[dy])
        return gather(wa1.at[dy], nx)

    def stage_b(dx):
        settle(wb1.at[dx, pl.ds(1, ny - 1)], rs_b1.at[dx])
        return gather(wb1.at[dx], ny)

    for step in sorted(range(1, ny), key=lambda o: -hops(o, ny)):
        wa2_out[step] = stage_a(step).astype(BF16)
        remote(wa2_out.at[step], wa2.at[step], ss_2.at[0], rs_2.at[0], at(step, 0, 0, 0)).start()
        wb2_out[step] = stage_b(step).astype(BF16)
        remote(wb2_out.at[step], wb2.at[step], ss_2.at[1], rs_2.at[1], at(0, step, 0, 0)).start()

    assign()

    first = stage_a(0)
    second = stage_b(0)
    settle(mass_in.at[pl.ds(1, chips - 1)], sem_m.at[1])
    mass = mass_in[0]
    for i in range(1, chips):
        mass = mass + mass_in[i]
    raw[width : width + 8, :] = jnp.broadcast_to(mass, (8, LANES))
    settle(wa2.at[pl.ds(1, ny - 1)], rs_2.at[0])
    for i in range(1, ny):
        first = first + wa2[i].astype(F32)
    raw[0:part, :] = first
    settle(wb2.at[pl.ds(1, nx - 1)], rs_2.at[1])
    for i in range(1, nx):
        second = second + wb2[i].astype(F32)
    raw[part:width, :] = second

    for i in range(ny):
        settle(wa1.at[i, pl.ds(1, nx - 1)], ss_a1.at[i])
    for i in range(nx):
        settle(wb1.at[i, pl.ds(1, ny - 1)], ss_b1.at[i])
    settle(wa2.at[pl.ds(1, ny - 1)], ss_2.at[0])
    settle(wb2.at[pl.ds(1, nx - 1)], ss_2.at[1])
    settle(mass_in.at[pl.ds(1, chips - 1)], sem_m.at[0])
    settle(slots_0.at[pl.ds(1, 2 * chips - 1)], sem_0.at[0])
    for it in range(ITERS - 1):
        settle(slots_c.at[it, pl.ds(1, chips - 1)], ssem_c.at[it])
    for it in range(ITERS):
        settle(slots_r.at[it, pl.ds(1, 2 * nz - 1)], ssem_r.at[it])


def write_out(assignment, raw, out, out_centers, centers, sems):
    pieces = 8
    size = assignment.shape[0] // pieces
    copies = [
        pltpu.make_async_copy(
            assignment.at[pl.ds(i * size, size)], out.at[pl.ds(i * size, size)], sems.at[i]
        )
        for i in range(pieces)
    ]
    for copy in copies:
        copy.start()
    width = centers.shape[1]
    scale = jnp.sqrt(F32(width)) / raw[width : width + 1, :]
    centers[...] = (raw[0:width, :] * scale).T
    copies.append(pltpu.make_async_copy(centers, out_centers, sems.at[pieces]))
    copies[-1].start()
    for copy in copies:
        copy.wait()


def solution(mesh):
    row_devices = mesh.shape["rows"]
    nz = mesh.shape["lists"]
    ny = nx = round((row_devices // 2) ** 0.5)

    def body(samples, centers):
        rows, width = samples.shape
        lists = centers.shape[0]
        half, chip_rows, chips = lists // 2, 2 * rows, ny * nx
        mc, mr = half // LANES, chip_rows // LANES
        part = width // 2
        dma = pltpu.SemaphoreType.DMA
        vmem = pl.BlockSpec(memory_space=pltpu.VMEM)
        hbm = pl.BlockSpec(memory_space=pl.ANY)
        big = ((rows, lists), BF16)
        small = ((lists // row_devices, width), F32)
        sums = ((width + 8, LANES), F32)
        assignment, raw = pl.pallas_call(
            functools.partial(
                kernel, ny, nx, nz, float(rows * row_devices), float(lists * nz)
            ),
            out_shape=(pltpu.VMEM(*big), pltpu.VMEM(*sums)),
            in_specs=[hbm, hbm],
            out_specs=(vmem, vmem),
            scratch_shapes=[
                pltpu.VMEM((rows, width), BF16),
                pltpu.VMEM((2, half // LANES, LANES, width), BF16),
                pltpu.VMEM((chip_rows, width), BF16),
                pltpu.VMEM((2, half, width), BF16),
                pltpu.VMEM((chip_rows, half), BF16),
                pltpu.VMEM((rows, half), BF16),
                pltpu.VMEM((half, chip_rows), BF16),
                pltpu.VMEM((width, chip_rows), F32),
                pltpu.VMEM((width + 16, chip_rows), BF16),
                pltpu.VMEM((max(half, chip_rows), LANES), F32),
                pltpu.VMEM((mc, LANES), F32),
                pltpu.VMEM((2, mc, LANES), BF16),
                pltpu.VMEM((2 * chips, mc, LANES), BF16),
                pltpu.VMEM((ITERS - 1, mc, LANES), F32),
                pltpu.VMEM((ITERS - 1, mc, LANES), BF16),
                pltpu.VMEM((ITERS - 1, chips, mc, LANES), BF16),
                pltpu.VMEM((ITERS, mr, LANES), F32),
                pltpu.VMEM((ITERS, mr, LANES), BF16),
                pltpu.VMEM((ITERS, 2 * nz, mr, LANES), BF16),
                pltpu.VMEM((mc, LANES), F32),
                pltpu.VMEM((mc, LANES), F32),
                pltpu.VMEM((chips, 1, LANES), F32),
                pltpu.VMEM((chips, 1, LANES), F32),
                pltpu.VMEM((chips, width, LANES), BF16),
                pltpu.VMEM((ny, nx, part, LANES), BF16),
                pltpu.VMEM((nx, ny, part, LANES), BF16),
                pltpu.VMEM((ny, part, LANES), BF16),
                pltpu.VMEM((nx, part, LANES), BF16),
                pltpu.VMEM((ny, part, LANES), BF16),
                pltpu.VMEM((nx, part, LANES), BF16),
                dma((3,)),
                dma((2,)),
                dma((ITERS - 1,)),
                dma((ITERS - 1,)),
                dma((ITERS,)),
                dma((ITERS,)),
                dma((2,)),
                dma((2,)),
                dma((2,)),
                dma((ny,)),
                dma((ny,)),
                dma((nx,)),
                dma((nx,)),
                dma((2,)),
                dma((2,)),
            ],
            compiler_params=pltpu.CompilerParams(
                collective_id=0, has_side_effects=True, vmem_limit_bytes=50 * 2**20
            ),
        )(samples, centers.reshape(half // LANES, 2, LANES, width))
        return tuple(
            pl.pallas_call(
                write_out,
                out_shape=(jax.ShapeDtypeStruct(*big), jax.ShapeDtypeStruct(*small)),
                in_specs=[vmem, vmem],
                out_specs=(hbm, hbm),
                scratch_shapes=[pltpu.VMEM(*small), dma((9,))],
                compiler_params=pltpu.CompilerParams(vmem_limit_bytes=2**20),
            )(
                pltpu.with_memory_space_constraint(assignment, pltpu.VMEM),
                pltpu.with_memory_space_constraint(raw, pltpu.VMEM),
            )
        )

    return jax.shard_map(
        body,
        mesh=mesh,
        in_specs=(P("rows", None), P("lists", None)),
        out_specs=(P("rows", "lists"), P(("lists", "rows"), None)),
        check_vma=False,
    )
```

```python
import functools

import jax
import jax.numpy as jnp
from jax import lax
from jax.experimental import pallas as pl
from jax.experimental.pallas import tpu as pltpu
from jax.sharding import PartitionSpec as P

ITERS = 3
SOFTMAX_TEMP_VALUE = 0.03
EXP2_SCALE = 1.0 / (SOFTMAX_TEMP_VALUE * 0.6931471805599453)
F32 = jnp.float32
BF16 = jnp.bfloat16
MESH = pl.DeviceIdType.MESH
NT = (((1,), (1,)), ((), ()))
LANES = 128


def unit_norm(block):
    wide = block.astype(F32)
    return (wide * lax.rsqrt(jnp.sum(wide * wide, 1, keepdims=True) + 1e-06)).astype(BF16)


def affinity(left, right):
    scores = lax.dot_general(left, right, NT, preferred_element_type=F32)
    return jnp.exp2(scores * EXP2_SCALE)


def hops(step, size):
    return min(step, size - step)


def kernel(
    ny, nx, nz, total_rows, total_lists,
    samples, centers, out, raw,
    xs, cs, uall, cn, km, ko, kt, ut, lhs_w, rcol, sums,
    msg_0, slots_0, own_c, msg_c, slots_c, own_r, msg_r, slots_r, list_own, list_in,
    mass_out, mass_in, w_out, wa1, wb1, wa2_out, wb2_out, wa2, wb2,
    ra, rb, ma, mb, in_sem, sem_0, ssem_c, rsem_c, ssem_r, rsem_r, sib_s, sib_r, sem_m,
    ss_a1, rs_a1, ss_b1, rs_b1, ss_2, rs_2, ss_f, rs_fa, rs_fb,
):
    rows, width = xs.shape
    half = cs.shape[1] * LANES
    chip_rows = 2 * rows
    chips = ny * nx
    part = width // 2

    place = lax.axis_index("rows")
    z = lax.axis_index("lists")
    y = place // (2 * nx)
    x = (place // 2) % nx
    c = place % 2
    other = 1 - c

    def at(dy, dx, dc, dz):
        return (
            (((y + dy) % ny) * nx + (x + dx) % nx) * 2 + (c + dc) % 2,
            (z + dz) % nz,
        )

    def remote(src, dst, ssem, rsem, target):
        return pltpu.make_async_remote_copy(
            src_ref=src, dst_ref=dst, send_sem=ssem, recv_sem=rsem,
            device_id=target, device_id_type=MESH,
        )

    def settle(ref, sem):
        pltpu.make_async_copy(ref, ref, sem).wait()

    sibling = at(0, 0, 1, 0)
    xy = [(dy, dx) for dy in range(ny) for dx in range(nx) if (dy, dx) != (0, 0)]
    xy.sort(key=lambda o: -(hops(o[0], ny) + hops(o[1], nx)))
    zc = [(dz, dc) for dz in range(nz) for dc in range(2) if (dz, dc) != (0, 0)]
    zc.sort(key=lambda o: -hops(o[0], nz))
    xyc = [(dy, dx, dc) for dy, dx in xy for dc in range(2)] + [(0, 0, 1)]

    loads = [
        pltpu.make_async_copy(samples, xs, in_sem.at[0]),
        pltpu.make_async_copy(centers.at[:, other], cs.at[1], in_sem.at[1]),
        pltpu.make_async_copy(centers.at[:, c], cs.at[0], in_sem.at[2]),
    ]
    for load in loads:
        load.start()

    barrier = pltpu.get_barrier_semaphore()
    for dy, dx, dc in xyc:
        pl.semaphore_signal(barrier, inc=1, device_id=at(dy, dx, dc, 0), device_id_type=MESH)
    for dz, dc in zc:
        if dz != 0:
            pl.semaphore_signal(
                barrier, inc=1, device_id=at(0, 0, dc, dz), device_id_type=MESH
            )

    own_rows = pl.ds(pl.multiple_of(c * rows, rows), rows)
    sib_rows = pl.ds(pl.multiple_of(other * rows, rows), rows)

    def to_rows(dst, vec):
        for i in range(dst.shape[0]):
            dst[i : i + 1, :] = vec[:, i * LANES : (i + 1) * LANES]

    def spread(compact):
        for i in range(compact.shape[0]):
            rcol[i * LANES : (i + 1) * LANES, :] = jnp.broadcast_to(
                compact[i : i + 1, :], (LANES, LANES)
            ).T

    def contract(compact, mat, dst):
        count = compact.shape[0]
        high = compact.astype(BF16).astype(F32)
        low = compact - high
        terms = [
            jnp.concatenate([term[i : i + 1, :] for i in range(count)], 1)
            for term in (high, low)
        ]
        terms.append(jnp.zeros((14, count * LANES), F32))
        lhs = jnp.concatenate(terms, 0).astype(BF16)
        got = jnp.dot(lhs, mat[...], preferred_element_type=F32)
        to_rows(dst, got[0:1, :] + got[1:2, :])

    def exchange_start(own, msg, slots, ssem, rsem, targets):
        msg[...] = own[...].astype(BF16)
        for slot, target in targets:
            remote(msg, slots.at[slot], ssem, rsem, target).start()

    def exchange_sum(own, slots, rsem, count):
        settle(slots.at[pl.ds(1, count - 1)], rsem)
        total = own[...]
        for i in range(1, count):
            total = total + slots[i].astype(F32)
        return total

    targets_c = [(dy * nx + dx, at(dy, dx, 0, 0)) for dy, dx in xy]
    targets_r = [(dz * 2 + dc, at(0, 0, dc, dz)) for dz, dc in zc]

    loads[0].wait()
    uall[own_rows, :] = unit_norm(xs[...])
    for which in (1, 0):
        loads[2 - which].wait()
        cn[which] = unit_norm(cs[which].reshape(half, width))
        block = affinity(uall[own_rows, :], cn[which])
        if which == 1:
            ko[...] = block.astype(BF16)
        else:
            km[own_rows, :] = block.astype(BF16)
        to_rows(sums, jnp.sum(block, 0, keepdims=True))
        msg_0[which] = sums[...].astype(BF16)
    pl.semaphore_wait(barrier, len(xyc) + 2 * (nz - 1))
    for dy, dx, dc in xyc:
        remote(
            msg_0.at[dc], slots_0.at[(dy * nx + dx) * 2 + dc], sem_0.at[0], sem_0.at[1],
            at(dy, dx, dc, 0),
        ).start()
    send_rows = remote(
        uall.at[own_rows], uall.at[own_rows], sib_s.at[0], sib_r.at[0], sibling
    )
    send_rows.start()
    kt[:, own_rows] = affinity(cn[0], uall[own_rows, :]).astype(BF16)
    send_rows.wait()
    kt[:, sib_rows] = affinity(cn[0], uall[sib_rows, :]).astype(BF16)

    send_lists = None
    row_scale = None
    for it in range(ITERS):
        if it == 0:
            column_total = exchange_sum(sums, slots_0, sem_0.at[1], 2 * chips)
        else:
            own, slots = own_c.at[it - 1], slots_c.at[it - 1]
            contract(row_scale, km, own)
            exchange_start(
                own, msg_c.at[it - 1], slots, ssem_c.at[it - 1], rsem_c.at[it - 1], targets_c
            )
            column_total = exchange_sum(own, slots, rsem_c.at[it - 1], chips)
        list_scale = 1.0 / (total_lists * column_total)
        if it == ITERS - 1:
            list_own[...] = list_scale
            send_lists = remote(list_own, list_in, sib_s.at[1], sib_r.at[1], sibling)
            send_lists.start()
        contract(list_scale, kt, own_r.at[it])
        exchange_start(
            own_r.at[it], msg_r.at[it], slots_r.at[it], ssem_r.at[it], rsem_r.at[it], targets_r
        )
        if it == 0:
            km[sib_rows, :] = affinity(uall[sib_rows, :], cn[0]).astype(BF16)
            ut[...] = uall[...].astype(F32).T
        row_total = exchange_sum(own_r.at[it], slots_r.at[it], rsem_r.at[it], 2 * nz)
        row_scale = 1.0 / (total_rows * row_total)

    index = lax.broadcasted_iota(jnp.int32, (16, LANES), 0)
    for i in range(chip_rows // LANES):
        lanes = pl.ds(i * LANES, LANES)
        one = row_scale[i : i + 1, :]
        lhs_w[0:width, lanes] = (ut[:, lanes] * one).astype(BF16)
        high = one.astype(BF16).astype(F32)
        lhs_w[width : width + 16, lanes] = jnp.where(
            index == 0, high, jnp.where(index == 1, one - high, 0.0)
        ).astype(BF16)

    merged = nx == 4
    hp = part // 2

    def reach(o):
        a, b = hops(o[0], ny), hops(o[1], nx)
        return -(4 * max(a, b) + a + b)

    def first_stage(piece, d, step_to, line, far, ssem, rsem, far_ssem, far_rsem):
        top, bottom = piece.at[pl.ds(0, hp)], piece.at[pl.ds(hp, hp)]
        if not merged:
            remote(piece, line.at[d], ssem, rsem, step_to(d)).start()
        elif d == 2:
            remote(top, far.at[0], far_ssem, far_rsem, step_to(1)).start()
            remote(bottom, far.at[1], far_ssem, far_rsem, step_to(3)).start()
        elif d == 1:
            remote(bottom, line.at[1, pl.ds(hp, hp)], ssem, rsem, step_to(1)).start()
        else:
            remote(top, line.at[2, pl.ds(0, hp)], ssem, rsem, step_to(3)).start()

    def merge(right, left, step_to, line, far, out_pieces, ssem, rsem, far_rsem):
        settle(far, far_rsem)
        out_pieces[0] = (right.astype(F32) + far[0].astype(F32)).astype(BF16)
        remote(
            out_pieces.at[0], line.at[1, pl.ds(0, hp)], ssem, rsem, step_to(1)
        ).start()
        out_pieces[1] = (left.astype(F32) + far[1].astype(F32)).astype(BF16)
        remote(
            out_pieces.at[1], line.at[2, pl.ds(hp, hp)], ssem, rsem, step_to(3)
        ).start()

    def along_x(d):
        return at(0, d, 0, 0)

    def along_y(d):
        return at(d, 0, 0, 0)

    order = sorted(xy + [(0, 0)], key=reach)
    cuts = list(range(0, chips + 1, 4))
    for low, high in zip(cuts[:-1], cuts[1:]):
        group = order[low:high]
        blocks = []
        for dy, dx in group:
            dest = ((y + dy) % ny) * nx + (x + dx) % nx
            blocks.append(km[:, pl.ds(pl.multiple_of(dest * LANES, LANES), LANES)])
        got = jnp.dot(
            lhs_w[...], jnp.concatenate(blocks, 1), preferred_element_type=F32
        )
        for n, (dy, dx) in enumerate(group):
            slot = dy * nx + dx
            piece = got[:, n * LANES : (n + 1) * LANES]
            first = wa1.at[dy, 0] if dx == 0 else w_out.at[slot, pl.ds(0, part)]
            second = wb1.at[dx, 0] if dy == 0 else w_out.at[slot, pl.ds(part, part)]
            first[...] = piece[0:part].astype(BF16)
            second[...] = piece[part:width].astype(BF16)
            if dx != 0:
                first_stage(
                    first, dx, along_x, wa1.at[dy], ra.at[dy], ss_a1.at[dy], rs_a1.at[dy],
                    ss_f.at[0], rs_fa.at[dy],
                )
            if dy != 0:
                first_stage(
                    second, dy, along_y, wb1.at[dx], rb.at[dx], ss_b1.at[dx], rs_b1.at[dx],
                    ss_f.at[1], rs_fb.at[dx],
                )
            mass = mass_in if slot == 0 else mass_out
            mass[slot] = piece[width : width + 1] + piece[width + 1 : width + 2]
            if slot != 0:
                remote(
                    mass_out.at[slot], mass_in.at[slot], sem_m.at[0], sem_m.at[1],
                    at(dy, dx, 0, 0),
                ).start()

    def assign(start, stop):
        for parity in range(2):
            @pl.when(c == parity)
            def _():
                def step(i, _):
                    here = pl.ds(pl.multiple_of(i * 16, 16), 16)
                    there = pl.ds(pl.multiple_of(parity * rows + i * 16, 16), 16)
                    scale = rcol[there, :]
                    for j in range(half // LANES):
                        lanes = pl.ds(j * LANES, LANES)
                        one = km[there, lanes].astype(F32) * scale * list_own[j : j + 1, :]
                        two = ko[here, lanes].astype(F32) * scale * list_in[j : j + 1, :]
                        out[here, pl.ds((2 * j + parity) * LANES, LANES)] = one.astype(BF16)
                        out[here, pl.ds((2 * j + 1 - parity) * LANES, LANES)] = two.astype(BF16)
                    return 0

                lax.fori_loop(start, stop, step, 0)

    steps = rows // 16
    if merged:
        for d in sorted(range(nx), key=lambda o: -hops(o, nx) if o else 0):
            merge(
                w_out[d * nx + 1, 0:hp, :], w_out[d * nx + 3, hp:part, :], along_x,
                wa1.at[d], ra.at[d], ma.at[d], ss_a1.at[d], rs_a1.at[d], rs_fa.at[d],
            )
            merge(
                w_out[nx + d, part : part + hp, :], w_out[3 * nx + d, part + hp : width, :],
                along_y, wb1.at[d], rb.at[d], mb.at[d], ss_b1.at[d], rs_b1.at[d], rs_fb.at[d],
            )
    spread(total_rows * row_scale)
    send_lists.wait()
    assign(0, steps // 2)
    line_count = 2 if merged else nx - 1
    line_slots = pl.ds(1, line_count)

    def gather(slots):
        total = slots[0].astype(F32)
        for i in range(1, 1 + line_count):
            total = total + slots[i].astype(F32)
        return total

    def stage_a(dy):
        settle(wa1.at[dy, line_slots], rs_a1.at[dy])
        return gather(wa1.at[dy])

    def stage_b(dx):
        settle(wb1.at[dx, line_slots], rs_b1.at[dx])
        return gather(wb1.at[dx])

    for step in sorted(range(1, ny), key=lambda o: -hops(o, ny)):
        wa2_out[step] = stage_a(step).astype(BF16)
        remote(wa2_out.at[step], wa2.at[step], ss_2.at[0], rs_2.at[0], at(step, 0, 0, 0)).start()
        wb2_out[step] = stage_b(step).astype(BF16)
        remote(wb2_out.at[step], wb2.at[step], ss_2.at[1], rs_2.at[1], at(0, step, 0, 0)).start()

    assign(steps // 2, steps)

    first = stage_a(0)
    second = stage_b(0)
    settle(mass_in.at[pl.ds(1, chips - 1)], sem_m.at[1])
    mass = mass_in[0]
    for i in range(1, chips):
        mass = mass + mass_in[i]
    raw[width : width + 8, :] = jnp.broadcast_to(mass, (8, LANES))
    settle(wa2.at[pl.ds(1, ny - 1)], rs_2.at[0])
    for i in range(1, ny):
        first = first + wa2[i].astype(F32)
    raw[0:part, :] = first
    settle(wb2.at[pl.ds(1, nx - 1)], rs_2.at[1])
    for i in range(1, nx):
        second = second + wb2[i].astype(F32)
    raw[part:width, :] = second

    for i in range(ny):
        settle(wa1.at[i, line_slots], ss_a1.at[i])
    for i in range(nx):
        settle(wb1.at[i, line_slots], ss_b1.at[i])
    settle(wa2.at[pl.ds(1, ny - 1)], ss_2.at[0])
    settle(wb2.at[pl.ds(1, nx - 1)], ss_2.at[1])
    if merged:
        settle(ra, ss_f.at[0])
        settle(rb, ss_f.at[1])
    settle(mass_in.at[pl.ds(1, chips - 1)], sem_m.at[0])
    settle(slots_0.at[pl.ds(1, 2 * chips - 1)], sem_0.at[0])
    for it in range(ITERS - 1):
        settle(slots_c.at[it, pl.ds(1, chips - 1)], ssem_c.at[it])
    for it in range(ITERS):
        settle(slots_r.at[it, pl.ds(1, 2 * nz - 1)], ssem_r.at[it])


def write_out(assignment, raw, out, out_centers, centers, sems):
    pieces = 8
    size = assignment.shape[0] // pieces
    copies = [
        pltpu.make_async_copy(
            assignment.at[pl.ds(i * size, size)], out.at[pl.ds(i * size, size)], sems.at[i]
        )
        for i in range(pieces)
    ]
    for copy in copies:
        copy.start()
    width = centers.shape[1]
    scale = jnp.sqrt(F32(width)) / raw[width : width + 1, :]
    centers[...] = (raw[0:width, :] * scale).T
    copies.append(pltpu.make_async_copy(centers, out_centers, sems.at[pieces]))
    copies[-1].start()
    for copy in copies:
        copy.wait()


def solution(mesh):
    row_devices = mesh.shape["rows"]
    nz = mesh.shape["lists"]
    ny = nx = round((row_devices // 2) ** 0.5)

    def body(samples, centers):
        rows, width = samples.shape
        lists = centers.shape[0]
        half, chip_rows, chips = lists // 2, 2 * rows, ny * nx
        mc, mr = half // LANES, chip_rows // LANES
        part = width // 2
        dma = pltpu.SemaphoreType.DMA
        vmem = pl.BlockSpec(memory_space=pltpu.VMEM)
        hbm = pl.BlockSpec(memory_space=pl.ANY)
        big = ((rows, lists), BF16)
        small = ((lists // row_devices, width), F32)
        sums = ((width + 8, LANES), F32)
        assignment, raw = pl.pallas_call(
            functools.partial(
                kernel, ny, nx, nz, float(rows * row_devices), float(lists * nz)
            ),
            out_shape=(pltpu.VMEM(*big), pltpu.VMEM(*sums)),
            in_specs=[hbm, hbm],
            out_specs=(vmem, vmem),
            scratch_shapes=[
                pltpu.VMEM((rows, width), BF16),
                pltpu.VMEM((2, half // LANES, LANES, width), BF16),
                pltpu.VMEM((chip_rows, width), BF16),
                pltpu.VMEM((2, half, width), BF16),
                pltpu.VMEM((chip_rows, half), BF16),
                pltpu.VMEM((rows, half), BF16),
                pltpu.VMEM((half, chip_rows), BF16),
                pltpu.VMEM((width, chip_rows), F32),
                pltpu.VMEM((width + 16, chip_rows), BF16),
                pltpu.VMEM((max(half, chip_rows), LANES), F32),
                pltpu.VMEM((mc, LANES), F32),
                pltpu.VMEM((2, mc, LANES), BF16),
                pltpu.VMEM((2 * chips, mc, LANES), BF16),
                pltpu.VMEM((ITERS - 1, mc, LANES), F32),
                pltpu.VMEM((ITERS - 1, mc, LANES), BF16),
                pltpu.VMEM((ITERS - 1, chips, mc, LANES), BF16),
                pltpu.VMEM((ITERS, mr, LANES), F32),
                pltpu.VMEM((ITERS, mr, LANES), BF16),
                pltpu.VMEM((ITERS, 2 * nz, mr, LANES), BF16),
                pltpu.VMEM((mc, LANES), F32),
                pltpu.VMEM((mc, LANES), F32),
                pltpu.VMEM((chips, 1, LANES), F32),
                pltpu.VMEM((chips, 1, LANES), F32),
                pltpu.VMEM((chips, width, LANES), BF16),
                pltpu.VMEM((ny, 3, part, LANES), BF16),
                pltpu.VMEM((nx, 3, part, LANES), BF16),
                pltpu.VMEM((ny, part, LANES), BF16),
                pltpu.VMEM((nx, part, LANES), BF16),
                pltpu.VMEM((ny, part, LANES), BF16),
                pltpu.VMEM((nx, part, LANES), BF16),
                pltpu.VMEM((ny, 2, part // 2, LANES), BF16),
                pltpu.VMEM((nx, 2, part // 2, LANES), BF16),
                pltpu.VMEM((ny, 2, part // 2, LANES), BF16),
                pltpu.VMEM((nx, 2, part // 2, LANES), BF16),
                dma((3,)),
                dma((2,)),
                dma((ITERS - 1,)),
                dma((ITERS - 1,)),
                dma((ITERS,)),
                dma((ITERS,)),
                dma((2,)),
                dma((2,)),
                dma((2,)),
                dma((ny,)),
                dma((ny,)),
                dma((nx,)),
                dma((nx,)),
                dma((2,)),
                dma((2,)),
                dma((2,)),
                dma((ny,)),
                dma((nx,)),
            ],
            compiler_params=pltpu.CompilerParams(
                collective_id=0, has_side_effects=True, vmem_limit_bytes=50 * 2**20
            ),
        )(samples, centers.reshape(half // LANES, 2, LANES, width))
        return tuple(
            pl.pallas_call(
                write_out,
                out_shape=(jax.ShapeDtypeStruct(*big), jax.ShapeDtypeStruct(*small)),
                in_specs=[vmem, vmem],
                out_specs=(hbm, hbm),
                scratch_shapes=[pltpu.VMEM(*small), dma((9,))],
                compiler_params=pltpu.CompilerParams(vmem_limit_bytes=2**20),
            )(
                pltpu.with_memory_space_constraint(assignment, pltpu.VMEM),
                pltpu.with_memory_space_constraint(raw, pltpu.VMEM),
            )
        )

    return jax.shard_map(
        body,
        mesh=mesh,
        in_specs=(P("rows", None), P("lists", None)),
        out_specs=(P("rows", "lists"), P(("lists", "rows"), None)),
        check_vma=False,
    )
```

```python
import functools

import jax
import jax.numpy as jnp
from jax import lax
from jax.experimental import pallas as pl
from jax.experimental.pallas import tpu as pltpu
from jax.sharding import PartitionSpec as P

ITERS = 3
SOFTMAX_TEMP_VALUE = 0.03
EXP2_SCALE = 1.0 / (SOFTMAX_TEMP_VALUE * 0.6931471805599453)
F32 = jnp.float32
BF16 = jnp.bfloat16
MESH = pl.DeviceIdType.MESH
NT = (((1,), (1,)), ((), ()))
LANES = 128


def unit_norm(block):
    wide = block.astype(F32)
    return (wide * lax.rsqrt(jnp.sum(wide * wide, 1, keepdims=True) + 1e-06)).astype(BF16)


def affinity(left, right):
    scores = lax.dot_general(left, right, NT, preferred_element_type=F32)
    return jnp.exp2(scores * EXP2_SCALE)


def hops(step, size):
    return min(step, size - step)


def kernel(
    ny, nx, nz, total_rows, total_lists,
    samples, centers, out, raw,
    xs, cs, uall, cn, km, ko, kt, ut, lhs_w, rcol, sums,
    msg_0, slots_0, own_c, msg_c, slots_c, own_r, msg_r, slots_r, list_own, list_in,
    mass_out, mass_in, w_out, wa1, wb1, wa2_out, wb2_out, wa2, wb2,
    ra, rb, ma, mb, in_sem, sem_0, ssem_c, rsem_c, ssem_r, rsem_r, sib_s, sib_r, sem_m,
    ss_a1, rs_a1, ss_b1, rs_b1, ss_2, rs_2, ss_f, rs_fa, rs_fb,
):
    rows, width = xs.shape
    half = cs.shape[1] * LANES
    chip_rows = 2 * rows
    chips = ny * nx
    part = width // 2

    place = lax.axis_index("rows")
    z = lax.axis_index("lists")
    y = place // (2 * nx)
    x = (place // 2) % nx
    c = place % 2
    other = 1 - c

    def at(dy, dx, dc, dz):
        return (
            (((y + dy) % ny) * nx + (x + dx) % nx) * 2 + (c + dc) % 2,
            (z + dz) % nz,
        )

    def remote(src, dst, ssem, rsem, target):
        return pltpu.make_async_remote_copy(
            src_ref=src, dst_ref=dst, send_sem=ssem, recv_sem=rsem,
            device_id=target, device_id_type=MESH,
        )

    def settle(ref, sem):
        pltpu.make_async_copy(ref, ref, sem).wait()

    sibling = at(0, 0, 1, 0)
    xy = [(dy, dx) for dy in range(ny) for dx in range(nx) if (dy, dx) != (0, 0)]
    xy.sort(key=lambda o: -(hops(o[0], ny) + hops(o[1], nx)))
    zc = [(dz, dc) for dz in range(nz) for dc in range(2) if (dz, dc) != (0, 0)]
    zc.sort(key=lambda o: -hops(o[0], nz))
    xyc = [(dy, dx, dc) for dy, dx in xy for dc in range(2)] + [(0, 0, 1)]

    loads = [
        pltpu.make_async_copy(samples, xs, in_sem.at[0]),
        pltpu.make_async_copy(centers.at[:, other], cs.at[1], in_sem.at[1]),
        pltpu.make_async_copy(centers.at[:, c], cs.at[0], in_sem.at[2]),
    ]
    for load in loads:
        load.start()

    barrier = pltpu.get_barrier_semaphore()
    for dy, dx, dc in xyc:
        pl.semaphore_signal(barrier, inc=1, device_id=at(dy, dx, dc, 0), device_id_type=MESH)
    for dz, dc in zc:
        if dz != 0:
            pl.semaphore_signal(
                barrier, inc=1, device_id=at(0, 0, dc, dz), device_id_type=MESH
            )

    own_rows = pl.ds(pl.multiple_of(c * rows, rows), rows)
    sib_rows = pl.ds(pl.multiple_of(other * rows, rows), rows)

    def to_rows(dst, vec):
        for i in range(dst.shape[0]):
            dst[i : i + 1, :] = vec[:, i * LANES : (i + 1) * LANES]

    def spread(compact):
        for i in range(compact.shape[0]):
            rcol[i * LANES : (i + 1) * LANES, :] = jnp.broadcast_to(
                compact[i : i + 1, :], (LANES, LANES)
            ).T

    def contract(compact, mat, dst):
        count = compact.shape[0]
        high = compact.astype(BF16).astype(F32)
        low = compact - high
        terms = [
            jnp.concatenate([term[i : i + 1, :] for i in range(count)], 1)
            for term in (high, low)
        ]
        terms.append(jnp.zeros((14, count * LANES), F32))
        lhs = jnp.concatenate(terms, 0).astype(BF16)
        got = jnp.dot(lhs, mat[...], preferred_element_type=F32)
        to_rows(dst, got[0:1, :] + got[1:2, :])

    def exchange_start(own, msg, slots, ssem, rsem, targets):
        msg[...] = own[...].astype(BF16)
        for slot, target in targets:
            remote(msg, slots.at[slot], ssem, rsem, target).start()

    def exchange_sum(own, slots, rsem, count):
        settle(slots.at[pl.ds(1, count - 1)], rsem)
        total = own[...]
        for i in range(1, count):
            total = total + slots[i].astype(F32)
        return total

    targets_c = [(dy * nx + dx, at(dy, dx, 0, 0)) for dy, dx in xy]
    targets_r = [(dz * 2 + dc, at(0, 0, dc, dz)) for dz, dc in zc]

    loads[0].wait()
    uall[own_rows, :] = unit_norm(xs[...])
    for which in (1, 0):
        loads[2 - which].wait()
        cn[which] = unit_norm(cs[which].reshape(half, width))
        block = affinity(uall[own_rows, :], cn[which])
        if which == 1:
            ko[...] = block.astype(BF16)
        else:
            km[own_rows, :] = block.astype(BF16)
        to_rows(sums, jnp.sum(block, 0, keepdims=True))
        msg_0[which] = sums[...].astype(BF16)
    pl.semaphore_wait(barrier, len(xyc) + 2 * (nz - 1))
    for dy, dx, dc in xyc:
        remote(
            msg_0.at[dc], slots_0.at[(dy * nx + dx) * 2 + dc], sem_0.at[0], sem_0.at[1],
            at(dy, dx, dc, 0),
        ).start()
    send_rows = remote(
        uall.at[own_rows], uall.at[own_rows], sib_s.at[0], sib_r.at[0], sibling
    )
    send_rows.start()
    kt[:, own_rows] = affinity(cn[0], uall[own_rows, :]).astype(BF16)
    send_rows.wait()
    kt[:, sib_rows] = affinity(cn[0], uall[sib_rows, :]).astype(BF16)

    send_lists = None
    row_scale = None
    for it in range(ITERS):
        if it == 0:
            column_total = exchange_sum(sums, slots_0, sem_0.at[1], 2 * chips)
        else:
            own, slots = own_c.at[it - 1], slots_c.at[it - 1]
            contract(row_scale, km, own)
            exchange_start(
                own, msg_c.at[it - 1], slots, ssem_c.at[it - 1], rsem_c.at[it - 1], targets_c
            )
            column_total = exchange_sum(own, slots, rsem_c.at[it - 1], chips)
        list_scale = 1.0 / (total_lists * column_total)
        if it == ITERS - 1:
            list_own[...] = list_scale
            send_lists = remote(list_own, list_in, sib_s.at[1], sib_r.at[1], sibling)
            send_lists.start()
        contract(list_scale, kt, own_r.at[it])
        exchange_start(
            own_r.at[it], msg_r.at[it], slots_r.at[it], ssem_r.at[it], rsem_r.at[it], targets_r
        )
        if it == 0:
            km[sib_rows, :] = affinity(uall[sib_rows, :], cn[0]).astype(BF16)
            ut[...] = uall[...].astype(F32).T
        row_total = exchange_sum(own_r.at[it], slots_r.at[it], rsem_r.at[it], 2 * nz)
        row_scale = 1.0 / (total_rows * row_total)

    index = lax.broadcasted_iota(jnp.int32, (16, LANES), 0)
    for i in range(chip_rows // LANES):
        lanes = pl.ds(i * LANES, LANES)
        one = row_scale[i : i + 1, :]
        lhs_w[0:width, lanes] = (ut[:, lanes] * one).astype(BF16)
        high = one.astype(BF16).astype(F32)
        lhs_w[width : width + 16, lanes] = jnp.where(
            index == 0, high, jnp.where(index == 1, one - high, 0.0)
        ).astype(BF16)

    merged = nx == 4
    hp = part // 2

    def reach(o):
        a, b = hops(o[0], ny), hops(o[1], nx)
        return -(4 * max(a, b) + a + b)

    def first_stage(piece, d, step_to, line, far, ssem, rsem, far_ssem, far_rsem):
        top, bottom = piece.at[pl.ds(0, hp)], piece.at[pl.ds(hp, hp)]
        if not merged:
            remote(piece, line.at[d], ssem, rsem, step_to(d)).start()
        elif d == 2:
            remote(top, far.at[0], far_ssem, far_rsem, step_to(1)).start()
            remote(bottom, far.at[1], far_ssem, far_rsem, step_to(3)).start()
        elif d == 1:
            remote(bottom, line.at[1, pl.ds(hp, hp)], ssem, rsem, step_to(1)).start()
        else:
            remote(top, line.at[2, pl.ds(0, hp)], ssem, rsem, step_to(3)).start()

    def merge(right, left, step_to, line, far, out_pieces, ssem, rsem, far_rsem):
        settle(far, far_rsem)
        out_pieces[0] = (right.astype(F32) + far[0].astype(F32)).astype(BF16)
        remote(
            out_pieces.at[0], line.at[1, pl.ds(0, hp)], ssem, rsem, step_to(1)
        ).start()
        out_pieces[1] = (left.astype(F32) + far[1].astype(F32)).astype(BF16)
        remote(
            out_pieces.at[1], line.at[2, pl.ds(hp, hp)], ssem, rsem, step_to(3)
        ).start()

    def along_x(d):
        return at(0, d, 0, 0)

    def along_y(d):
        return at(d, 0, 0, 0)

    order = sorted(xy + [(0, 0)], key=reach)
    cuts = list(range(0, chips + 1, 4))
    for low, high in zip(cuts[:-1], cuts[1:]):
        group = order[low:high]
        blocks = []
        for dy, dx in group:
            dest = ((y + dy) % ny) * nx + (x + dx) % nx
            blocks.append(km[:, pl.ds(pl.multiple_of(dest * LANES, LANES), LANES)])
        got = jnp.dot(
            lhs_w[...], jnp.concatenate(blocks, 1), preferred_element_type=F32
        )
        for n, (dy, dx) in enumerate(group):
            slot = dy * nx + dx
            piece = got[:, n * LANES : (n + 1) * LANES]
            first = wa1.at[dy, 0] if dx == 0 else w_out.at[slot, pl.ds(0, part)]
            second = wb1.at[dx, 0] if dy == 0 else w_out.at[slot, pl.ds(part, part)]
            first[...] = piece[0:part].astype(BF16)
            second[...] = piece[part:width].astype(BF16)
            if dx != 0:
                first_stage(
                    first, dx, along_x, wa1.at[dy], ra.at[dy], ss_a1.at[dy], rs_a1.at[dy],
                    ss_f.at[0], rs_fa.at[dy],
                )
            if dy != 0:
                first_stage(
                    second, dy, along_y, wb1.at[dx], rb.at[dx], ss_b1.at[dx], rs_b1.at[dx],
                    ss_f.at[1], rs_fb.at[dx],
                )
            mass = mass_in if slot == 0 else mass_out
            mass[slot] = piece[width : width + 1] + piece[width + 1 : width + 2]
            if slot != 0:
                remote(
                    mass_out.at[slot], mass_in.at[slot], sem_m.at[0], sem_m.at[1],
                    at(dy, dx, 0, 0),
                ).start()

    def assign(start, stop):
        for parity in range(2):
            @pl.when(c == parity)
            def _():
                def step(i, _):
                    here = pl.ds(pl.multiple_of(i * 16, 16), 16)
                    there = pl.ds(pl.multiple_of(parity * rows + i * 16, 16), 16)
                    scale = rcol[there, :]
                    for j in range(half // LANES):
                        lanes = pl.ds(j * LANES, LANES)
                        one = km[there, lanes].astype(F32) * scale * list_own[j : j + 1, :]
                        two = ko[here, lanes].astype(F32) * scale * list_in[j : j + 1, :]
                        out[here, pl.ds((2 * j + parity) * LANES, LANES)] = one.astype(BF16)
                        out[here, pl.ds((2 * j + 1 - parity) * LANES, LANES)] = two.astype(BF16)
                    return 0

                lax.fori_loop(start, stop, step, 0)

    steps = rows // 16
    if merged:
        for d in sorted(range(nx), key=lambda o: -hops(o, nx) if o else 0):
            merge(
                w_out[d * nx + 1, 0:hp, :], w_out[d * nx + 3, hp:part, :], along_x,
                wa1.at[d], ra.at[d], ma.at[d], ss_a1.at[d], rs_a1.at[d], rs_fa.at[d],
            )
            merge(
                w_out[nx + d, part : part + hp, :], w_out[3 * nx + d, part + hp : width, :],
                along_y, wb1.at[d], rb.at[d], mb.at[d], ss_b1.at[d], rs_b1.at[d], rs_fb.at[d],
            )
    spread(total_rows * row_scale)
    send_lists.wait()
    assign(0, steps // 2)
    line_count = 2 if merged else nx - 1
    line_slots = pl.ds(1, line_count)

    def gather(slots):
        total = slots[0].astype(F32)
        for i in range(1, 1 + line_count):
            total = total + slots[i].astype(F32)
        return total

    def stage_a(dy):
        settle(wa1.at[dy, line_slots], rs_a1.at[dy])
        return gather(wa1.at[dy])

    def stage_b(dx):
        settle(wb1.at[dx, line_slots], rs_b1.at[dx])
        return gather(wb1.at[dx])

    for step in sorted(range(1, ny), key=lambda o: -hops(o, ny)):
        wa2_out[step] = stage_a(step).astype(BF16)
        remote(wa2_out.at[step], wa2.at[step], ss_2.at[0], rs_2.at[0], at(step, 0, 0, 0)).start()
        wb2_out[step] = stage_b(step).astype(BF16)
        remote(wb2_out.at[step], wb2.at[step], ss_2.at[1], rs_2.at[1], at(0, step, 0, 0)).start()

    assign(steps // 2, steps)

    for i in range(ny):
        settle(wa1.at[i, line_slots], ss_a1.at[i])
    for i in range(nx):
        settle(wb1.at[i, line_slots], ss_b1.at[i])
    if merged:
        settle(ra, ss_f.at[0])
        settle(rb, ss_f.at[1])
    settle(mass_in.at[pl.ds(1, chips - 1)], sem_m.at[0])
    settle(slots_0.at[pl.ds(1, 2 * chips - 1)], sem_0.at[0])
    for it in range(ITERS - 1):
        settle(slots_c.at[it, pl.ds(1, chips - 1)], ssem_c.at[it])
    for it in range(ITERS):
        settle(slots_r.at[it, pl.ds(1, 2 * nz - 1)], ssem_r.at[it])

    first = stage_a(0)
    second = stage_b(0)
    settle(mass_in.at[pl.ds(1, chips - 1)], sem_m.at[1])
    mass = mass_in[0]
    for i in range(1, chips):
        mass = mass + mass_in[i]
    raw[width : width + 8, :] = jnp.broadcast_to(mass, (8, LANES))
    settle(wa2.at[pl.ds(1, ny - 1)], rs_2.at[0])
    for i in range(1, ny):
        first = first + wa2[i].astype(F32)
    raw[0:part, :] = first
    settle(wb2.at[pl.ds(1, nx - 1)], rs_2.at[1])
    for i in range(1, nx):
        second = second + wb2[i].astype(F32)
    raw[part:width, :] = second
    settle(wa2.at[pl.ds(1, ny - 1)], ss_2.at[0])
    settle(wb2.at[pl.ds(1, nx - 1)], ss_2.at[1])


def write_out(assignment, raw, out, out_centers, centers, sems):
    pieces = 8
    size = assignment.shape[0] // pieces
    copies = [
        pltpu.make_async_copy(
            assignment.at[pl.ds(i * size, size)], out.at[pl.ds(i * size, size)], sems.at[i]
        )
        for i in range(pieces)
    ]
    for copy in copies:
        copy.start()
    width = centers.shape[1]
    scale = jnp.sqrt(F32(width)) / raw[width : width + 1, :]
    centers[...] = (raw[0:width, :] * scale).T
    copies.append(pltpu.make_async_copy(centers, out_centers, sems.at[pieces]))
    copies[-1].start()
    for copy in copies:
        copy.wait()


def solution(mesh):
    row_devices = mesh.shape["rows"]
    nz = mesh.shape["lists"]
    ny = nx = round((row_devices // 2) ** 0.5)

    def body(samples, centers):
        rows, width = samples.shape
        lists = centers.shape[0]
        half, chip_rows, chips = lists // 2, 2 * rows, ny * nx
        mc, mr = half // LANES, chip_rows // LANES
        part = width // 2
        dma = pltpu.SemaphoreType.DMA
        vmem = pl.BlockSpec(memory_space=pltpu.VMEM)
        hbm = pl.BlockSpec(memory_space=pl.ANY)
        big = ((rows, lists), BF16)
        small = ((lists // row_devices, width), F32)
        sums = ((width + 8, LANES), F32)
        assignment, raw = pl.pallas_call(
            functools.partial(
                kernel, ny, nx, nz, float(rows * row_devices), float(lists * nz)
            ),
            out_shape=(pltpu.VMEM(*big), pltpu.VMEM(*sums)),
            in_specs=[hbm, hbm],
            out_specs=(vmem, vmem),
            scratch_shapes=[
                pltpu.VMEM((rows, width), BF16),
                pltpu.VMEM((2, half // LANES, LANES, width), BF16),
                pltpu.VMEM((chip_rows, width), BF16),
                pltpu.VMEM((2, half, width), BF16),
                pltpu.VMEM((chip_rows, half), BF16),
                pltpu.VMEM((rows, half), BF16),
                pltpu.VMEM((half, chip_rows), BF16),
                pltpu.VMEM((width, chip_rows), F32),
                pltpu.VMEM((width + 16, chip_rows), BF16),
                pltpu.VMEM((max(half, chip_rows), LANES), F32),
                pltpu.VMEM((mc, LANES), F32),
                pltpu.VMEM((2, mc, LANES), BF16),
                pltpu.VMEM((2 * chips, mc, LANES), BF16),
                pltpu.VMEM((ITERS - 1, mc, LANES), F32),
                pltpu.VMEM((ITERS - 1, mc, LANES), BF16),
                pltpu.VMEM((ITERS - 1, chips, mc, LANES), BF16),
                pltpu.VMEM((ITERS, mr, LANES), F32),
                pltpu.VMEM((ITERS, mr, LANES), BF16),
                pltpu.VMEM((ITERS, 2 * nz, mr, LANES), BF16),
                pltpu.VMEM((mc, LANES), F32),
                pltpu.VMEM((mc, LANES), F32),
                pltpu.VMEM((chips, 1, LANES), F32),
                pltpu.VMEM((chips, 1, LANES), F32),
                pltpu.VMEM((chips, width, LANES), BF16),
                pltpu.VMEM((ny, 3, part, LANES), BF16),
                pltpu.VMEM((nx, 3, part, LANES), BF16),
                pltpu.VMEM((ny, part, LANES), BF16),
                pltpu.VMEM((nx, part, LANES), BF16),
                pltpu.VMEM((ny, part, LANES), BF16),
                pltpu.VMEM((nx, part, LANES), BF16),
                pltpu.VMEM((ny, 2, part // 2, LANES), BF16),
                pltpu.VMEM((nx, 2, part // 2, LANES), BF16),
                pltpu.VMEM((ny, 2, part // 2, LANES), BF16),
                pltpu.VMEM((nx, 2, part // 2, LANES), BF16),
                dma((3,)),
                dma((2,)),
                dma((ITERS - 1,)),
                dma((ITERS - 1,)),
                dma((ITERS,)),
                dma((ITERS,)),
                dma((2,)),
                dma((2,)),
                dma((2,)),
                dma((ny,)),
                dma((ny,)),
                dma((nx,)),
                dma((nx,)),
                dma((2,)),
                dma((2,)),
                dma((2,)),
                dma((ny,)),
                dma((nx,)),
            ],
            compiler_params=pltpu.CompilerParams(
                collective_id=0, has_side_effects=True, vmem_limit_bytes=50 * 2**20
            ),
        )(samples, centers.reshape(half // LANES, 2, LANES, width))
        return tuple(
            pl.pallas_call(
                write_out,
                out_shape=(jax.ShapeDtypeStruct(*big), jax.ShapeDtypeStruct(*small)),
                in_specs=[vmem, vmem],
                out_specs=(hbm, hbm),
                scratch_shapes=[pltpu.VMEM(*small), dma((9,))],
                compiler_params=pltpu.CompilerParams(vmem_limit_bytes=2**20),
            )(
                pltpu.with_memory_space_constraint(assignment, pltpu.VMEM),
                pltpu.with_memory_space_constraint(raw, pltpu.VMEM),
            )
        )

    return jax.shard_map(
        body,
        mesh=mesh,
        in_specs=(P("rows", None), P("lists", None)),
        out_specs=(P("rows", "lists"), P(("lists", "rows"), None)),
        check_vma=False,
    )
```
